32 devices in a mesh: slab: 2 (over x), chan: 16 (over z, y, core).
Axes of the slice: x: 2, y: 2, z: 4, core: 2. Of those that a mesh axis runs over, the one named last changes fastest.
Arguments:
- cube: float32 [128, 128, 256], P(('slab', 'chan')), parts along dimension 0, may hold values from -8 to 8
- multipliers: int32 [6, 4], replicated, may hold values from 1 to 5
- noise_code: int32 [128, 6, 4], P(('slab', 'chan')), parts along dimension 0, may hold values from 16 to 511
Outputs:
- denoised: float32 [128, 128, 256], P(('slab', 'chan')), parts along dimension 0
The draws below stay inside these ranges and needn't reach their ends.
There are 2 independent parts, one for each index of `slab`. The reference program is written for one: setup_inputs(seed, part) draws one part's arguments, and reference() takes and returns one part's arrays. A program takes and returns all parts, laid end to end along the dimension named above; an argument that names none is the same for every part. Nothing has to cross between parts.
All inputs are finite; a program needn't handle non-finite values.
Results may differ from the reference program's by a relative error of at most 0.00002.
Values sent between devices are 32-bit elements; how exact they have to be, the bound alone decides.
No kernel may reach another device: no remote copies, remote signals or barrier semaphores. Data moves between devices by JAX's collectives and lax.ppermute only.
A program may use at most 64 MiB of HBM per device.

```python
import jax
import jax.numpy as jnp
from jax import lax

ROWS = 128
COLS = 256
SCALES_XY = 5
SCALES_NU = 3
CHANNELS = 64


def with_ends(entries, rng, low, top_value):
    index_at = [jax.random.randint(jax.random.fold_in(rng, axis), (), 0, length) for axis, length in enumerate(entries.shape)]
    widest = entries.shape.index(max(entries.shape))
    neighbour = index_at[:widest] + [(index_at[widest] + 1) % entries.shape[widest]] + index_at[widest + 1:]
    return entries.at[tuple(index_at)].set(low).at[tuple(neighbour)].set(top_value)


def block_levels(own_key, dims, cuts, least, high):
    gain, own = 1.0, jax.random.fold_in(own_key, 6)
    for position, blocks in cuts:
        draws = jnp.exp(jax.random.uniform(jax.random.fold_in(own, position), (blocks,), jnp.float32, least / len(cuts), high / len(cuts)))
        gain = gain * jnp.repeat(draws, dims[position] // blocks).reshape([-1 if axis == position else 1 for axis in range(len(dims))])
    return gain


def centred(stream_key, dims, deviation, bound, shards=(), held_as=jnp.bfloat16):
    factor_of = block_levels(stream_key, dims, shards, -0.22, 0.18) if shards else 1.0
    values = jax.random.normal(stream_key, dims, jnp.float32) * deviation * factor_of
    return jnp.minimum(jnp.maximum(values, -bound), bound).astype(held_as)


def setup_inputs(seed: int = 0, part: int = 0) -> dict:
    streams_of = jax.random.split(jax.random.key(seed), 4)
    own_keys = jax.random.split(jax.random.fold_in(streams_of[3], part), 4)
    cube = centred(own_keys[0], (CHANNELS, ROWS, COLS), 1.0, 8.0, ((0, 16),), jnp.float32)
    multipliers = with_ends(jax.random.randint(streams_of[1], (SCALES_XY + 1, SCALES_NU + 1), 1, 6), jax.random.fold_in(streams_of[1], 1), 1, 5).astype(jnp.int32)
    noise_code = with_ends(jax.random.randint(own_keys[2], (CHANNELS, SCALES_XY + 1, SCALES_NU + 1), 16, 512), jax.random.fold_in(own_keys[2], 1), 16, 511).astype(jnp.int32)
    return dict(cube=cube, multipliers=multipliers, noise_code=noise_code)


SPLINE = (0.0625, 0.25, 0.375, 0.25, 0.0625)
level_step = 1.0 / 1024.0


def smooth(field, axis, step):
    widths = [(0, 0)] * field.ndim
    widths[axis] = (2 * step, 2 * step)
    padded = jnp.pad(field, widths)
    length = field.shape[axis]
    total = jnp.zeros(field.shape, jnp.float32)
    for place, weight in enumerate(SPLINE):
        total = total + weight * lax.slice_in_dim(padded, place * step, place * step + length, axis=axis)
    return total


def shrink(value, limit):
    return value - jnp.clip(value, -limit, limit)


def reference(cube, multipliers, noise_code):
    level = multipliers.astype(jnp.float32)[None] * noise_code.astype(jnp.float32) * level_step
    smoothed = cube
    total = jnp.zeros(cube.shape, jnp.float32)
    for j in range(SCALES_XY + 1):
        if j < SCALES_XY:
            step = 2 ** j
            following = smooth(smooth(smoothed, 1, step), 2, step)
            band = smoothed - following
        else:
            band = smoothed
        current = band
        for s in range(SCALES_NU):
            coarse = smooth(current, 0, 2 ** s)
            total = total + shrink(current - coarse, level[:, j, s][:, None, None])
            current = coarse
        if j < SCALES_XY:
            total = total + shrink(current, level[:, j, SCALES_NU][:, None, None])
            smoothed = following
        else:
            total = total + current
    return total
```

```python
import functools

import jax
import jax.numpy as jnp
import numpy as np
from jax import lax
from jax.experimental import pallas as pl
from jax.experimental.pallas import tpu as pltpu
from jax.sharding import PartitionSpec as P

SCALES_XY = 5
SCALES_NU = 3
TAPS = (1, 4, 6, 4, 1)
REACH = 14
F32 = jnp.float32
BF16 = jnp.bfloat16


def pairs(count, distance, phase):
    out = []
    for i in range(count):
        j = i + distance if (i // distance) % 2 == phase else i - distance
        if 0 <= j < count:
            out.append((i, j))
    return out


def column_matrices(cols):
    place = np.arange(cols)
    offset = place[None, :] - place[:, None]
    mats = []
    for j in range(SCALES_XY):
        m = np.zeros((cols, cols), np.float32)
        for k, w in enumerate(TAPS):
            m += np.where(offset == (k - 2) * 2**j, np.float32(w / 256.0), np.float32(0))
        mats.append(m)
    return jnp.asarray(np.stack(mats), BF16)


def prep_kernel(half, core_ref, cube, got, v8, za, zb, sem):
    core = core_ref[0]
    mine = cube.at[:, pl.ds(pl.multiple_of(core * half, half), half)]

    def move(dst, k, which):
        block = k // 2
        part = pl.ds((k % 2) * 2, 2)

        @pl.when(core == block)
        def _():
            pltpu.make_async_copy(mine.at[part], dst, sem.at[which]).start()

        @pl.when(core != block)
        def _():
            pltpu.make_async_copy(got.at[part], dst, sem.at[which]).start()

    n = 0
    ends = []
    for k in range(4):
        move(v8.at[pl.ds(2 * k, 2)], k, n)
        ends.append((v8.at[pl.ds(2 * k, 2)], n))
        n += 1
    for z, first in ((za, core_ref[1]), (zb, core_ref[2])):
        for k in range(3):
            dst = z.at[pl.ds(2 * k, 2)]
            move(dst, first + k, n)
            ends.append((dst, n))
            n += 1
    for dst, which in ends:
        pltpu.make_async_copy(got.at[pl.ds(0, 2)], dst, sem.at[which]).wait()


def b3(a, b, c, d, e):
    return 0.375 * c + 0.25 * (b + d) + 0.0625 * (a + e)


def spectral_kernel(half, cols, place_ref, v8, e2, o2, e4, o4, own, other, ext, sem):
    chip = 8
    copies = [
        pltpu.make_async_copy(v8, ext.at[pl.ds(REACH, chip)], sem.at[0]),
        pltpu.make_async_copy(e2, ext.at[pl.ds(place_ref[1], chip)], sem.at[1]),
        pltpu.make_async_copy(o2, ext.at[pl.ds(place_ref[2], chip)], sem.at[2]),
        pltpu.make_async_copy(e4, ext.at[pl.ds(place_ref[3], 6)], sem.at[3]),
        pltpu.make_async_copy(o4, ext.at[pl.ds(place_ref[4], 6)], sem.at[4]),
    ]
    for c in copies:
        c.start()
    for c in copies:
        c.wait()
    core = place_ref[0]
    first = place_ref[5]
    channels = place_ref[6]
    inside = {}
    for k in range(-12, 20):
        if k < 0 or k >= chip:
            at = first + k
            inside[k] = jnp.where((at >= 0) & (at < channels), 1.0, 0.0).astype(F32)

    def body(r, carry):
        rows = pl.ds(pl.multiple_of(r * 8, 8), 8)
        for half_cols in range(cols // 128):
            lanes = pl.ds(half_cols * 128, 128)
            x = {k: ext[k + REACH, rows, lanes] for k in range(-14, 22)}

            def smooth(v, lo, hi, step):
                out = {}
                for k in range(lo, hi):
                    y = b3(*(v[k + o * step] for o in (-2, -1, 0, 1, 2)))
                    out[k] = y * inside[k] if k in inside else y
                return out

            c1 = smooth(x, -12, 20, 1)
            c2 = smooth(c1, -8, 16, 2)
            c3 = smooth(c2, 0, 8, 4)
            for s, c in enumerate((c1, c2, c3)):
                for k in range(4):
                    a, b = c[k], c[k + 4]
                    own[s, k, rows, lanes] = jnp.where(core == 0, a, b)
                    other[s, k, rows, lanes] = jnp.where(core == 0, b, a)
        return carry

    lax.fori_loop(0, half // 8, body, 0)


def spatial_kernel(rows, cols, core_ref, mult, noise, cube, own, got, mats, out, a, p, acc):
    i = pl.program_id(0)
    half = rows // 2
    pad = 2 ** SCALES_XY
    core = core_ref[0]
    mine_at = pl.multiple_of(core * half, half)
    got_at = pl.multiple_of((1 - core) * half, half)

    @pl.when(i == 0)
    def _():
        p[:, :pad] = jnp.zeros((4, pad, cols), F32)
        p[:, pad + rows :] = jnp.zeros((4, pad, cols), F32)

    a[3, pl.ds(mine_at, half)] = own[2, 0]
    a[3, pl.ds(got_at, half)] = got[2, 0]
    for s in (1, 2):
        a[s, pl.ds(mine_at, half)] = own[s - 1, 0] - own[s, 0]
        a[s, pl.ds(got_at, half)] = got[s - 1, 0] - got[s, 0]
    a[0, pl.ds(mine_at, half)] = cube[0, pl.ds(mine_at, half)] - own[0, 0]
    a[0, pl.ds(got_at, half)] = cube[0, pl.ds(got_at, half)] - got[0, 0]

    chunk = 32

    def limit(j, s):
        return (mult[j, s] * noise[i, j, s]).astype(F32) * (1.0 / 1024.0)

    for j in range(SCALES_XY):
        d = 2**j
        w = mats[j]
        for s in range(4):
            x = a[s]
            hi = x.astype(BF16)
            lo = (x - hi.astype(F32)).astype(BF16)
            p[s, pl.ds(pad, rows)] = jnp.dot(hi, w, preferred_element_type=F32) + jnp.dot(lo, w, preferred_element_type=F32)
        for r in range(0, rows, chunk):
            total = None
            for s in range(4):
                at = pad + r
                c0 = p[s, pl.ds(at, chunk)]
                c1 = p[s, pl.ds(at - d, chunk)] + p[s, pl.ds(at + d, chunk)]
                c2 = p[s, pl.ds(at - 2 * d, chunk)] + p[s, pl.ds(at + 2 * d, chunk)]
                nxt = 6.0 * c0 + 4.0 * c1 + c2
                b = a[s, pl.ds(r, chunk)] - nxt
                a[s, pl.ds(r, chunk)] = nxt
                lim = limit(j, s)
                v = b - jnp.clip(b, -lim, lim)
                total = v if total is None else total + v
            if j == 0:
                acc[pl.ds(r, chunk)] = total
            else:
                acc[pl.ds(r, chunk)] += total
    for r in range(0, rows, chunk):
        total = acc[pl.ds(r, chunk)] + a[3, pl.ds(r, chunk)]
        for s in range(3):
            b = a[s, pl.ds(r, chunk)]
            lim = limit(SCALES_XY, s)
            total = total + (b - jnp.clip(b, -lim, lim))
        out[0, pl.ds(r, chunk)] = total


def per_device(count, cube, multipliers, noise_code):
    local, rows, cols = cube.shape
    assert local == 4 and count % 2 == 0 and rows % 128 == 0
    half = rows // 2
    chip = 2 * local
    me = lax.axis_index("chan").astype(jnp.int32)
    core = me % 2
    g2 = (me // 2) % 2
    g4 = (me // 4) % 2

    def permute(v, distance, phase):
        return lax.ppermute(v, "chan", pairs(count, distance, phase))

    smem = pl.BlockSpec(memory_space=pltpu.SMEM)
    anyspace = pl.BlockSpec(memory_space=pl.ANY)
    vmem = pl.BlockSpec(memory_space=pltpu.VMEM)
    got = permute(lax.dynamic_slice_in_dim(cube, (1 - core) * half, half, 1), 1, 0)
    prep_at = jnp.stack([core, 1 - g4, g4])
    v8, za, zb = pl.pallas_call(
        functools.partial(prep_kernel, half),
        in_specs=[smem, anyspace, anyspace],
        out_specs=[anyspace] * 3,
        out_shape=[jax.ShapeDtypeStruct((n, half, cols), F32) for n in (chip, 6, 6)],
        scratch_shapes=[pltpu.SemaphoreType.DMA((10,))],
        name="prep",
    )(prep_at, cube, got)
    e2 = permute(v8, 2, 0)
    o2 = permute(v8, 2, 1)
    e4 = permute(za, 4, 0)
    o4 = permute(zb, 4, 1)
    place = jnp.stack(
        [
            core,
            jnp.where(g2 == 0, 22, 6),
            jnp.where(g2 == 0, 6, 22),
            jnp.where(g4 == 0, 30, 0),
            jnp.where(g4 == 0, 0, 30),
            (me // 2) * chip,
            jnp.int32(count * local),
        ]
    ).astype(jnp.int32)
    own, other = pl.pallas_call(
        functools.partial(spectral_kernel, half, cols),
        in_specs=[smem] + [anyspace] * 5,
        out_specs=[vmem] * 2,
        out_shape=[jax.ShapeDtypeStruct((3, local, half, cols), F32)] * 2,
        scratch_shapes=[pltpu.VMEM((chip + 2 * REACH, half, cols), F32), pltpu.SemaphoreType.DMA((5,))],
        compiler_params=pltpu.CompilerParams(vmem_limit_bytes=32 * 2**20),
        name="spectral",
    )(place, v8, e2, o2, e4, o4)
    back = permute(other, 1, 0)
    pad = 2**SCALES_XY
    plane = pl.BlockSpec((1, rows, cols), lambda i: (i, 0, 0))
    third = pl.BlockSpec((3, 1, half, cols), lambda i: (0, i, 0, 0))
    return pl.pallas_call(
        functools.partial(spatial_kernel, rows, cols),
        grid=(local,),
        in_specs=[smem, smem, smem, plane, third, third, pl.BlockSpec((SCALES_XY, cols, cols), lambda i: (0, 0, 0))],
        out_specs=plane,
        out_shape=jax.ShapeDtypeStruct(cube.shape, F32),
        scratch_shapes=[
            pltpu.VMEM((4, rows, cols), F32),
            pltpu.VMEM((4, rows + 2 * pad, cols), F32),
            pltpu.VMEM((rows, cols), F32),
        ],
        compiler_params=pltpu.CompilerParams(vmem_limit_bytes=32 * 2**20),
        name="spatial",
    )(core[None], multipliers, noise_code, cube, own, back, column_matrices(cols))


def solution(mesh):
    placed = (P(("slab", "chan"), None, None), P(), P(("slab", "chan"), None, None))
    return jax.shard_map(
        functools.partial(per_device, mesh.shape["chan"]),
        mesh=mesh,
        in_specs=placed,
        out_specs=P(("slab", "chan"), None, None),
        check_vma=False,
    )
```

```python
import functools

import jax
import jax.numpy as jnp
import numpy as np
from jax import lax
from jax.experimental import pallas as pl
from jax.experimental.pallas import tpu as pltpu
from jax.sharding import PartitionSpec as P

SCALES_XY = 5
SCALES_NU = 3
TAPS = (1, 4, 6, 4, 1)
REACH = 14
LANES = 128
EDGE = 8
F32 = jnp.float32
BF16 = jnp.bfloat16


def pairs(count, distance, phase):
    out = []
    for i in range(count):
        j = i + distance if (i // distance) % 2 == phase else i - distance
        if 0 <= j < count:
            out.append((i, j))
    return out


def column_matrices(cols):
    place = np.arange(cols)
    offset = place[None, :] - place[:, None]
    mats = []
    for j in range(SCALES_XY):
        m = np.zeros((cols, cols), np.float32)
        for k, w in enumerate(TAPS):
            m += np.where(offset == (k - 2) * 2**j, np.float32(w / 256.0), np.float32(0))
        mats.append(m)
    return jnp.asarray(np.stack(mats), BF16)


def plus(*terms):
    terms = [t for t in terms if t is not None]
    out = terms[0]
    for t in terms[1:]:
        out = out + t
    return out


def pick(values, k):
    return values[k] if 0 <= k < len(values) else None


def spline4(values, first, step, lo, hi):
    cur = dict(enumerate(values, first))
    for shift in (-1, -1, 1, 1):
        cur = {k: v + cur[k + shift * step] for k, v in cur.items() if k + shift * step in cur}
    return [cur[k] for k in range(lo, hi)]


def split(x):
    hi = x.astype(BF16)
    return hi, (x - hi.astype(F32)).astype(BF16)


def denoise_kernel(rows, cols, local, pieces, place, mult, noise, *refs):
    ins = refs[:pieces]
    mats, out = refs[pieces : pieces + 2]
    ext, detail, a, p, acc, done, sem, out_sem = refs[pieces + 2 :]
    halves = cols // LANES
    groups = rows // 8
    centre = 5 * local
    copies = [
        pltpu.make_async_copy(ref, ext.at[pl.ds(place[2 + n], ref.shape[0])], sem.at[n])
        for n, ref in enumerate(ins)
    ]
    for c in copies:
        c.start()
    for s in range(SCALES_NU + 1):
        for h in range(halves):
            p[s, h, :EDGE] = jnp.zeros((EDGE, LANES), F32)
            p[s, h, EDGE + rows :] = jnp.zeros((EDGE, LANES), F32)
    first, channels = place[0], place[1]
    inside = {}
    for k in list(range(-12, 0)) + list(range(local, local + 12)):
        at = first + k
        inside[k] = jnp.where((at >= 0) & (at < channels), 1.0, 0.0).astype(F32)
    for c in copies:
        c.wait()

    def spectral(g, carry):
        r = pl.ds(pl.multiple_of(g * 8, 8), 8)
        for h in range(halves):
            lanes = pl.ds(h * LANES, LANES)
            x = [ext[centre + k, r, lanes] for k in range(-REACH, local + REACH)]
            c1 = spline4(x, -14, 1, -12, local + 12)
            c1 = [v * inside[k] if k in inside else v for k, v in enumerate(c1, -12)]
            c2 = spline4(c1, -12, 2, -8, local + 8)
            c2 = [v * inside[k] if k in inside else v for k, v in enumerate(c2, -8)]
            c3 = spline4(c2, -8, 4, 0, local)
            for k in range(local):
                e0 = x[k + 14]
                e1 = c1[k + 12] * (1.0 / 16.0)
                e2 = c2[k + 8] * (1.0 / 256.0)
                e3 = c3[k] * (1.0 / 4096.0)
                detail[k, 0, h, r] = e0 - e1
                detail[k, 1, h, r] = e1 - e2
                detail[k, 2, h, r] = e2 - e3
                detail[k, 3, h, r] = e3
        return carry

    lax.fori_loop(0, groups, spectral, 0)

    def spatial(i, carry):
        def limit(j, s):
            return (mult[s, j] * noise[i, s, j]).astype(F32) * (1.0 / 1024.0)

        def shrink(v, j, s):
            lim = limit(j, s)
            return v - jnp.clip(v, -lim, lim)

        def source(j, s):
            return detail.at[i, s] if j == 0 else a.at[s]

        def columns(j, s):
            src = source(j, s)
            hi, lo = split(jnp.concatenate([src[h] for h in range(halves)], 1))
            y = jnp.dot(jnp.concatenate([hi, lo], 0), mats[j], preferred_element_type=F32)
            y = y[:rows] + y[rows:]
            for h in range(halves):
                p[s, h, pl.ds(EDGE, rows)] = y[:, h * LANES : (h + 1) * LANES]

        def smooth_rows(j, s, h):
            d = 2**j

            def load(o):
                return [p[s, h, pl.ds(EDGE + 8 * k + o, 8)] for k in range(groups)]

            x = load(0)
            if d >= 8:
                q = d // 8
                cur = x
                for _ in range(4):
                    cur = [plus(pick(cur, k), pick(cur, k - q)) for k in range(len(cur) + q)]
                return cur[2 * q : 2 * q + groups]
            if d == 4:
                u = [p[s, h, pl.ds(EDGE + 8 * k - 4, 8)] for k in range(groups + 1)]
                near = [u[k] + u[k + 1] for k in range(groups)]
                far = [plus(pick(x, k - 1), pick(x, k + 1)) for k in range(groups)]
            elif d == 2:
                u = [p[s, h, pl.ds(EDGE + 8 * k - 4, 8)] for k in range(groups + 1)]
                near = [m + n for m, n in zip(load(-2), load(2))]
                far = [u[k] + u[k + 1] for k in range(groups)]
            else:
                near = [m + n for m, n in zip(load(-1), load(1))]
                far = [m + n for m, n in zip(load(-2), load(2))]
            return [6.0 * x[k] + 4.0 * near[k] + far[k] for k in range(groups)]

        for j in range(SCALES_XY):
            for s in range(SCALES_NU + 1):
                columns(j, s)
            for h in range(halves):
                total = [None] * groups
                for s in range(SCALES_NU + 1):
                    src = source(j, s)
                    y = smooth_rows(j, s, h)
                    for k in range(groups):
                        r = pl.ds(8 * k, 8)
                        v = shrink(src[h, r] - y[k], j, s)
                        a[s, h, r] = y[k]
                        total[k] = plus(total[k], v)
                for k in range(groups):
                    r = pl.ds(8 * k, 8)
                    if j == 0:
                        acc[h, r] = total[k]
                    else:
                        acc[h, r] += total[k]
        for h in range(halves):
            total = acc[h] + a[SCALES_NU, h]
            for s in range(SCALES_NU):
                total = total + shrink(a[s, h], SCALES_XY, s)
            done[i, :, h * LANES : (h + 1) * LANES] = total
        pltpu.make_async_copy(done.at[i], out.at[i], out_sem.at[i]).start()
        return carry

    lax.fori_loop(0, local, spatial, 0)
    for i in range(local):
        pltpu.make_async_copy(done.at[i], out.at[i], out_sem.at[i]).wait()


def per_device(count, cube, multipliers, noise_code):
    local, rows, cols = cube.shape
    assert local == 4 and count % 2 == 0 and rows % 8 == 0 and cols % LANES == 0
    me = lax.axis_index("chan").astype(jnp.int32)
    core = me % 2
    g2 = (me // 2) % 2
    g4 = (me // 4) % 2
    beside = 1 - 2 * core

    def permute(v, distance, phase):
        return lax.ppermute(v, "chan", pairs(count, distance, phase))

    pieces = [(cube, 0)]
    for distance, group in ((2, g2), (4, g4)):
        for phase in (0, 1):
            up = jnp.where(group == phase, 1, -1)
            pieces.append((permute(cube, distance, phase), up * distance))
    pieces += [(permute(v, 1, 0), at + beside) for v, at in pieces]
    place = jnp.stack([me * local, jnp.int32(count * local)] + [(5 + at) * local for _, at in pieces]).astype(jnp.int32)
    smem = pl.BlockSpec(memory_space=pltpu.SMEM)
    vmem = pl.BlockSpec(memory_space=pltpu.VMEM)
    plane = (cols // LANES, rows, LANES)
    scales = SCALES_NU + 1
    return pl.pallas_call(
        functools.partial(denoise_kernel, rows, cols, local, len(pieces)),
        in_specs=[smem] * 3 + [vmem] * (len(pieces) + 1),
        out_specs=pl.BlockSpec(memory_space=pltpu.HBM),
        out_shape=jax.ShapeDtypeStruct(cube.shape, F32),
        scratch_shapes=[
            pltpu.VMEM((11 * local, rows, cols), F32),
            pltpu.VMEM((local, scales) + plane, F32),
            pltpu.VMEM((scales,) + plane, F32),
            pltpu.VMEM((scales, cols // LANES, rows + 2 * EDGE, LANES), F32),
            pltpu.VMEM(plane, F32),
            pltpu.VMEM((local, rows, cols), F32),
            pltpu.SemaphoreType.DMA((len(pieces),)),
            pltpu.SemaphoreType.DMA((local,)),
        ],
        compiler_params=pltpu.CompilerParams(vmem_limit_bytes=18 * 2**20),
        name="denoise",
    )(place, multipliers.T, noise_code.transpose(0, 2, 1), *[v for v, _ in pieces], column_matrices(cols))


def solution(mesh):
    placed = (P(("slab", "chan"), None, None), P(), P(("slab", "chan"), None, None))
    return jax.shard_map(
        functools.partial(per_device, mesh.shape["chan"]),
        mesh=mesh,
        in_specs=placed,
        out_specs=P(("slab", "chan"), None, None),
        check_vma=False,
    )
```

```python
import functools

import jax
import jax.numpy as jnp
from jax import lax
from jax.experimental import pallas as pl
from jax.experimental.pallas import tpu as pltpu
from jax.sharding import PartitionSpec as P

SCALES_XY = 5
SCALES_NU = 3
TAPS = (1, 4, 6, 4, 1)
REACH = 14
LANES = 128
EDGE = 8
F32 = jnp.float32
BF16 = jnp.bfloat16


def pairs(count, distance, phase):
    out = []
    for i in range(count):
        j = i + distance if (i // distance) % 2 == phase else i - distance
        if 0 <= j < count:
            out.append((i, j))
    return out


def plus(*terms):
    terms = [t for t in terms if t is not None]
    out = terms[0]
    for t in terms[1:]:
        out = out + t
    return out


def pick(values, k):
    return values[k] if 0 <= k < len(values) else None


def spline4(values, first, step, lo, hi):
    cur = dict(enumerate(values, first))
    for shift in (-1, -1, 1, 1):
        cur = {k: v + cur[k + shift * step] for k, v in cur.items() if k + shift * step in cur}
    return [cur[k] for k in range(lo, hi)]


def split(x):
    hi = x.astype(BF16)
    return hi, (x - hi.astype(F32)).astype(BF16)


def denoise_kernel(rows, cols, local, pieces, place, mult, noise, *refs):
    ins = refs[:pieces]
    mats, out = refs[pieces : pieces + 2]
    ext, detail, a, p, acc, done, sem, out_sem = refs[pieces + 2 :]
    halves = cols // LANES
    groups = rows // 8
    centre = 4 * local
    copies = [
        pltpu.make_async_copy(ref, ext.at[pl.ds(place[2 + n], ref.shape[0])], sem.at[n])
        for n, ref in enumerate(ins)
    ]
    for c in copies:
        c.start()
    for s in range(SCALES_NU + 1):
        for h in range(halves):
            p[s, h, :EDGE] = jnp.zeros((EDGE, LANES), F32)
            p[s, h, EDGE + rows :] = jnp.zeros((EDGE, LANES), F32)
    first, channels = place[0], place[1]
    inside = {}
    for k in list(range(-12, 0)) + list(range(local, local + 12)):
        at = first + k
        inside[k] = jnp.where((at >= 0) & (at < channels), 1.0, 0.0).astype(F32)
    for c in copies:
        c.wait()

    def spectral(g, carry):
        r = pl.ds(pl.multiple_of(g * 8, 8), 8)
        for h in range(halves):
            lanes = pl.ds(h * LANES, LANES)
            x = [ext[centre + k, r, lanes] for k in range(-REACH, local + REACH)]
            c1 = spline4(x, -14, 1, -12, local + 12)
            c1 = [v * inside[k] if k in inside else v for k, v in enumerate(c1, -12)]
            c2 = spline4(c1, -12, 2, -8, local + 8)
            c2 = [v * inside[k] if k in inside else v for k, v in enumerate(c2, -8)]
            c3 = spline4(c2, -8, 4, 0, local)
            for k in range(local):
                e0 = x[k + 14]
                e1 = c1[k + 12] * (1.0 / 16.0)
                e2 = c2[k + 8] * (1.0 / 256.0)
                e3 = c3[k] * (1.0 / 4096.0)
                detail[k, 0, h, r] = e0 - e1
                detail[k, 1, h, r] = e1 - e2
                detail[k, 2, h, r] = e2 - e3
                detail[k, 3, h, r] = e3
        return carry

    lax.fori_loop(0, groups, spectral, 0)

    def spatial(i, carry):
        def limit(j, s):
            return (mult[s, j] * noise[i, s, j]).astype(F32) * (1.0 / 1024.0)

        def shrink(v, j, s):
            lim = limit(j, s)
            return v - jnp.clip(v, -lim, lim)

        def source(j, s):
            return detail.at[i, s] if j == 0 else a.at[s]

        def columns(j, s):
            src = source(j, s)
            hi, lo = split(jnp.concatenate([src[h] for h in range(halves)], 1))
            y = jnp.dot(jnp.concatenate([hi, lo], 0), mats[j], preferred_element_type=F32)
            y = y[:rows] + y[rows:]
            for h in range(halves):
                p[s, h, pl.ds(EDGE, rows)] = y[:, h * LANES : (h + 1) * LANES]

        def smooth_rows(j, s, h):
            d = 2**j

            def load(o):
                return [p[s, h, pl.ds(EDGE + 8 * k + o, 8)] for k in range(groups)]

            x = load(0)
            if d >= 8:
                q = d // 8
                cur = x
                for _ in range(4):
                    cur = [plus(pick(cur, k), pick(cur, k - q)) for k in range(len(cur) + q)]
                return cur[2 * q : 2 * q + groups]
            if d == 4:
                u = [p[s, h, pl.ds(EDGE + 8 * k - 4, 8)] for k in range(groups + 1)]
                near = [u[k] + u[k + 1] for k in range(groups)]
                far = [plus(pick(x, k - 1), pick(x, k + 1)) for k in range(groups)]
            elif d == 2:
                u = [p[s, h, pl.ds(EDGE + 8 * k - 4, 8)] for k in range(groups + 1)]
                near = [m + n for m, n in zip(load(-2), load(2))]
                far = [u[k] + u[k + 1] for k in range(groups)]
            else:
                near = [m + n for m, n in zip(load(-1), load(1))]
                far = [m + n for m, n in zip(load(-2), load(2))]
            return [6.0 * x[k] + 4.0 * near[k] + far[k] for k in range(groups)]

        for j in range(SCALES_XY):
            for s in range(SCALES_NU + 1):
                columns(j, s)
            for h in range(halves):
                total = [None] * groups
                for s in range(SCALES_NU + 1):
                    src = source(j, s)
                    y = smooth_rows(j, s, h)
                    for k in range(groups):
                        r = pl.ds(8 * k, 8)
                        v = shrink(src[h, r] - y[k], j, s)
                        a[s, h, r] = y[k]
                        total[k] = plus(total[k], v)
                for k in range(groups):
                    r = pl.ds(8 * k, 8)
                    if j == 0:
                        acc[h, r] = total[k]
                    else:
                        acc[h, r] += total[k]
        for h in range(halves):
            total = acc[h] + a[SCALES_NU, h]
            for s in range(SCALES_NU):
                total = total + shrink(a[s, h], SCALES_XY, s)
            done[i, :, h * LANES : (h + 1) * LANES] = total
        pltpu.make_async_copy(done.at[i], out.at[i], out_sem.at[i]).start()
        return carry

    lax.fori_loop(0, local, spatial, 0)
    for i in range(local):
        pltpu.make_async_copy(done.at[i], out.at[i], out_sem.at[i]).wait()


def setup_kernel(cols, cube, copy, mats, sem):
    fetch = pltpu.make_async_copy(cube, copy, sem)
    fetch.start()
    row = lax.broadcasted_iota(jnp.int32, (cols, cols), 0)
    offset = lax.broadcasted_iota(jnp.int32, (cols, cols), 1) - row
    for j in range(SCALES_XY):
        m = jnp.zeros((cols, cols), F32)
        for k, w in enumerate(TAPS):
            m = jnp.where(offset == (k - 2) * 2**j, w / 256.0, m)
        mats[j] = m.astype(BF16)
    fetch.wait()


def per_device(count, cube, multipliers, noise_code):
    local, rows, cols = cube.shape
    assert local == 4 and count % 2 == 0 and rows % 8 == 0 and cols % LANES == 0
    me = lax.axis_index("chan").astype(jnp.int32)
    core = me % 2
    g2 = (me // 2) % 2
    g4 = (me // 4) % 2
    beside = 1 - 2 * core
    smem = pl.BlockSpec(memory_space=pltpu.SMEM)
    hbm = pl.BlockSpec(memory_space=pltpu.HBM)
    vmem = pl.BlockSpec(memory_space=pltpu.VMEM)
    anyspace = pl.BlockSpec(memory_space=pl.ANY)

    def permute(v, distance, phase):
        return lax.ppermute(v, "chan", pairs(count, distance, phase))

    relay = [(i, i + 4) for i in range(count - 4) if (i // 2) % 2 == 0]
    relay += [(i, i - 4) for i in range(4, count) if (i // 2) % 2 == 1]
    cut = local // 2
    near = permute(cube, 2, 0)
    two_a = permute(cube, 4, 0)
    two_b = permute(cube, 4, 1)
    far_hi = permute(cube[cut:], 2, 1)
    far_lo = lax.ppermute(near[:cut], "chan", relay)
    here, mats = pl.pallas_call(
        functools.partial(setup_kernel, cols),
        in_specs=[anyspace],
        out_specs=[vmem] * 2,
        out_shape=[jax.ShapeDtypeStruct(cube.shape, F32), jax.ShapeDtypeStruct((SCALES_XY, cols, cols), BF16)],
        scratch_shapes=[pltpu.SemaphoreType.DMA],
        compiler_params=pltpu.CompilerParams(vmem_limit_bytes=4 * 2**20),
        cost_estimate=pl.CostEstimate(flops=10**7, bytes_accessed=2 * 10**6, transcendentals=0),
        name="setup",
    )(cube)
    two_a, two_b, near, here, mats = lax.optimization_barrier((two_a, two_b, near, here, mats))
    far_hi, far_lo = lax.optimization_barrier((far_hi, far_lo))
    up2 = jnp.where(g2 == 0, 2, -2)
    up4 = jnp.where(g4 == 0, 4, -4)
    pieces = [(here, 0, 0), (near, up2, 0), (two_a, up4, 0), (two_b, -up4, 0), (far_hi, -up2, cut), (far_lo, -up2, 0)]
    pieces += [(permute(cube if n == 0 else v, 1, 0), at + beside, o) for n, (v, at, o) in enumerate(pieces)]
    place = [jnp.where(abs(at) > 4, 9, at + 4) * local + o for _, at, o in pieces]
    place = jnp.stack([me * local, jnp.int32(count * local)] + place).astype(jnp.int32)
    plane = (cols // LANES, rows, LANES)
    scales = SCALES_NU + 1
    return pl.pallas_call(
        functools.partial(denoise_kernel, rows, cols, local, len(pieces)),
        in_specs=[smem] * 3 + [anyspace] * len(pieces) + [vmem],
        out_specs=hbm,
        out_shape=jax.ShapeDtypeStruct(cube.shape, F32),
        scratch_shapes=[
            pltpu.VMEM((10 * local, rows, cols), F32),
            pltpu.VMEM((local, scales) + plane, F32),
            pltpu.VMEM((scales,) + plane, F32),
            pltpu.VMEM((scales, cols // LANES, rows + 2 * EDGE, LANES), F32),
            pltpu.VMEM(plane, F32),
            pltpu.VMEM((local, rows, cols), F32),
            pltpu.SemaphoreType.DMA((len(pieces),)),
            pltpu.SemaphoreType.DMA((local,)),
        ],
        compiler_params=pltpu.CompilerParams(vmem_limit_bytes=11 * 2**20),
        name="denoise",
    )(place, multipliers.T, noise_code.transpose(0, 2, 1), *[v for v, _, _ in pieces], mats)


def solution(mesh):
    placed = (P(("slab", "chan"), None, None), P(), P(("slab", "chan"), None, None))
    return jax.shard_map(
        functools.partial(per_device, mesh.shape["chan"]),
        mesh=mesh,
        in_specs=placed,
        out_specs=P(("slab", "chan"), None, None),
        check_vma=False,
    )
```

```python
import functools

import jax
import jax.numpy as jnp
from jax import lax
from jax.experimental import pallas as pl
from jax.experimental.pallas import tpu as pltpu
from jax.sharding import PartitionSpec as P

SCALES_XY = 5
SCALES_NU = 3
TAPS = (1, 4, 6, 4, 1)
REACH = 14
LANES = 128
EDGE = 8
F32 = jnp.float32
BF16 = jnp.bfloat16


def pairs(count, distance, phase):
    out = []
    for i in range(count):
        j = i + distance if (i // distance) % 2 == phase else i - distance
        if 0 <= j < count:
            out.append((i, j))
    return out


def plus(*terms):
    terms = [t for t in terms if t is not None]
    out = terms[0]
    for t in terms[1:]:
        out = out + t
    return out


def pick(values, k):
    return values[k] if 0 <= k < len(values) else None


def spline4(values, first, step, lo, hi):
    cur = dict(enumerate(values, first))
    for shift in (-1, -1, 1, 1):
        cur = {k: v + cur[k + shift * step] for k, v in cur.items() if k + shift * step in cur}
    return [cur[k] for k in range(lo, hi)]


def split(x):
    hi = x.astype(BF16)
    return hi, (x - hi.astype(F32)).astype(BF16)


def denoise_kernel(rows, cols, local, count, mult, noise, *refs):
    pieces = 12
    ins = refs[:pieces]
    mats, out = refs[pieces : pieces + 2]
    detail, a, p, acc, done, out_sem = refs[pieces + 2 :]
    halves = cols // LANES
    groups = rows // 8
    me = lax.axis_index("chan").astype(jnp.int32)
    for s in range(SCALES_NU + 1):
        for h in range(halves):
            p[s, h, :EDGE] = jnp.zeros((EDGE, LANES), F32)
            p[s, h, EDGE + rows :] = jnp.zeros((EDGE, LANES), F32)
    def spectral(where, inside, g, carry):
        r = pl.ds(pl.multiple_of(g * 8, 8), 8)
        for h in range(halves):
            lanes = pl.ds(h * LANES, LANES)
            x = [where[k][0][where[k][1], r, lanes] for k in range(-REACH, local + REACH)]
            c1 = spline4(x, -14, 1, -12, local + 12)
            c1 = [v * inside[k] if k in inside else v for k, v in enumerate(c1, -12)]
            c2 = spline4(c1, -12, 2, -8, local + 8)
            c2 = [v * inside[k] if k in inside else v for k, v in enumerate(c2, -8)]
            c3 = spline4(c2, -8, 4, 0, local)
            for k in range(local):
                e0 = x[k + 14]
                e1 = c1[k + 12] * (1.0 / 16.0)
                e2 = c2[k + 8] * (1.0 / 256.0)
                e3 = c3[k] * (1.0 / 4096.0)
                detail[k, 0, h, r] = e0 - e1
                detail[k, 1, h, r] = e1 - e2
                detail[k, 2, h, r] = e2 - e3
                detail[k, 3, h, r] = e3
        return carry

    for turn in range(8):
        beside = 1 - 2 * (turn % 2)
        up2 = 2 - 4 * (turn // 2 % 2)
        up4 = 4 - 8 * (turn // 4)
        held = [(0, 0), (up2, 0), (up4, 0), (-up4, 0), (-up2, local // 2), (-up2, 0)]
        held += [(block + beside, o) for block, o in held]
        where = {}
        for (block, o), ref in zip(held, ins):
            for k in range(ref.shape[0]):
                where[block * local + o + k] = (ref, k)

        @pl.when(me % 8 == turn)
        def _():
            inside = {}
            for k in range(-12, -local * turn):
                inside[k] = (me > turn).astype(F32)
            for k in range(local * (8 - turn), local + 12):
                inside[k] = (me < count - 8 + turn).astype(F32)
            lax.fori_loop(0, groups, functools.partial(spectral, where, inside), 0)

    def spatial(i, carry):
        def limits(j, s):
            level = jnp.full((8, LANES), (mult[s, j] * noise[i, s, j]).astype(F32) * (1.0 / 1024.0))
            return -level, level

        def shrink(v, ends):
            return v - jnp.minimum(jnp.maximum(v, ends[0]), ends[1])

        def source(j, s):
            return detail.at[i, s] if j == 0 else a.at[s]

        def columns(j, s):
            src = source(j, s)
            hi, lo = split(jnp.concatenate([src[h] for h in range(halves)], 1))
            y = jnp.dot(jnp.concatenate([hi, lo], 0), mats[j], preferred_element_type=F32)
            y = y[:rows] + y[rows:]
            for h in range(halves):
                p[s, h, pl.ds(EDGE, rows)] = y[:, h * LANES : (h + 1) * LANES]

        def smooth_rows(j, s, h):
            d = 2**j

            def load(o):
                return [p[s, h, pl.ds(EDGE + 8 * k + o, 8)] for k in range(groups)]

            x = load(0)
            if d >= 8:
                q = d // 8
                cur = x
                for _ in range(4):
                    cur = [plus(pick(cur, k), pick(cur, k - q)) for k in range(len(cur) + q)]
                return cur[2 * q : 2 * q + groups]
            if d == 4:
                u = [p[s, h, pl.ds(EDGE + 8 * k - 4, 8)] for k in range(groups + 1)]
                near = [u[k] + u[k + 1] for k in range(groups)]
                far = [plus(pick(x, k - 1), pick(x, k + 1)) for k in range(groups)]
            elif d == 2:
                u = [p[s, h, pl.ds(EDGE + 8 * k - 4, 8)] for k in range(groups + 1)]
                near = [m + n for m, n in zip(load(-2), load(2))]
                far = [u[k] + u[k + 1] for k in range(groups)]
            else:
                near = [m + n for m, n in zip(load(-1), load(1))]
                far = [m + n for m, n in zip(load(-2), load(2))]
            return [6.0 * x[k] + 4.0 * near[k] + far[k] for k in range(groups)]

        for j in range(SCALES_XY):
            ends = [limits(j, s) for s in range(SCALES_NU + 1)]
            for s in range(SCALES_NU + 1):
                columns(j, s)
            for h in range(halves):
                total = [None] * groups
                for s in range(SCALES_NU + 1):
                    src = source(j, s)
                    y = smooth_rows(j, s, h)
                    for k in range(groups):
                        r = pl.ds(8 * k, 8)
                        v = shrink(src[h, r] - y[k], ends[s])
                        a[s, h, r] = y[k]
                        total[k] = plus(total[k], v)
                for k in range(groups):
                    r = pl.ds(8 * k, 8)
                    if j == 0:
                        acc[h, r] = total[k]
                    else:
                        acc[h, r] += total[k]
        ends = [limits(SCALES_XY, s) for s in range(SCALES_NU)]
        for h in range(halves):
            for k in range(groups):
                r = pl.ds(8 * k, 8)
                total = acc[h, r] + a[SCALES_NU, h, r]
                for s in range(SCALES_NU):
                    total = total + shrink(a[s, h, r], ends[s])
                done[i, r, h * LANES : (h + 1) * LANES] = total
        pltpu.make_async_copy(done.at[i], out.at[i], out_sem.at[i]).start()
        return carry

    lax.fori_loop(0, local, spatial, 0)
    for i in range(local):
        pltpu.make_async_copy(done.at[i], out.at[i], out_sem.at[i]).wait()


def setup_kernel(cols, cube, copy, mats, sem):
    fetch = pltpu.make_async_copy(cube, copy, sem)
    fetch.start()
    row = lax.broadcasted_iota(jnp.int32, (cols, cols), 0)
    offset = lax.broadcasted_iota(jnp.int32, (cols, cols), 1) - row
    for j in range(SCALES_XY):
        m = jnp.zeros((cols, cols), F32)
        for k, w in enumerate(TAPS):
            m = jnp.where(offset == (k - 2) * 2**j, w / 256.0, m)
        mats[j] = m.astype(BF16)
    fetch.wait()


def per_device(count, cube, multipliers, noise_code):
    local, rows, cols = cube.shape
    assert local == 4 and count % 8 == 0 and rows % 8 == 0 and cols % LANES == 0
    smem = pl.BlockSpec(memory_space=pltpu.SMEM)
    hbm = pl.BlockSpec(memory_space=pltpu.HBM)
    vmem = pl.BlockSpec(memory_space=pltpu.VMEM)
    anyspace = pl.BlockSpec(memory_space=pl.ANY)

    def permute(v, distance, phase):
        return lax.ppermute(v, "chan", pairs(count, distance, phase))

    relay = [(i, i + 4) for i in range(count - 4) if (i // 2) % 2 == 0]
    relay += [(i, i - 4) for i in range(4, count) if (i // 2) % 2 == 1]
    cut = local // 2
    near = permute(cube, 2, 0)
    two_a = permute(cube, 4, 0)
    two_b = permute(cube, 4, 1)
    far_hi = permute(cube[cut:], 2, 1)
    far_lo = lax.ppermute(near[:cut], "chan", relay)
    here, mats = pl.pallas_call(
        functools.partial(setup_kernel, cols),
        in_specs=[anyspace],
        out_specs=[vmem] * 2,
        out_shape=[jax.ShapeDtypeStruct(cube.shape, F32), jax.ShapeDtypeStruct((SCALES_XY, cols, cols), BF16)],
        scratch_shapes=[pltpu.SemaphoreType.DMA],
        compiler_params=pltpu.CompilerParams(vmem_limit_bytes=4 * 2**20),
        cost_estimate=pl.CostEstimate(flops=10**7, bytes_accessed=2 * 10**6, transcendentals=0),
        name="setup",
    )(cube)
    two_a, two_b, near, here, mats = lax.optimization_barrier((two_a, two_b, near, here, mats))
    far_hi, far_lo = lax.optimization_barrier((far_hi, far_lo))
    pieces = [here, near, two_a, two_b, far_hi, far_lo]
    pieces += [permute(cube if n == 0 else v, 1, 0) for n, v in enumerate(pieces)]
    plane = (cols // LANES, rows, LANES)
    scales = SCALES_NU + 1
    return pl.pallas_call(
        functools.partial(denoise_kernel, rows, cols, local, count),
        in_specs=[smem] * 2 + [vmem] * len(pieces) + [vmem],
        out_specs=hbm,
        out_shape=jax.ShapeDtypeStruct(cube.shape, F32),
        scratch_shapes=[
            pltpu.VMEM((local, scales) + plane, F32),
            pltpu.VMEM((scales,) + plane, F32),
            pltpu.VMEM((scales, cols // LANES, rows + 2 * EDGE, LANES), F32),
            pltpu.VMEM(plane, F32),
            pltpu.VMEM((local, rows, cols), F32),
            pltpu.SemaphoreType.DMA((local,)),
        ],
        compiler_params=pltpu.CompilerParams(vmem_limit_bytes=11 * 2**20),
        name="denoise",
    )(multipliers.T, noise_code.transpose(0, 2, 1), *pieces, mats)


def solution(mesh):
    placed = (P(("slab", "chan"), None, None), P(), P(("slab", "chan"), None, None))
    return jax.shard_map(
        functools.partial(per_device, mesh.shape["chan"]),
        mesh=mesh,
        in_specs=placed,
        out_specs=P(("slab", "chan"), None, None),
        check_vma=False,
    )
```

```python
import functools

import jax
import jax.numpy as jnp
import numpy as np
from jax import lax
from jax.experimental import pallas as pl
from jax.experimental.pallas import tpu as pltpu
from jax.sharding import PartitionSpec as P

SCALES_XY = 5
SCALES_NU = 3
TAPS = (1, 4, 6, 4, 1)
REACH = 14
LANES = 128
EDGE = 8
F32 = jnp.float32
BF16 = jnp.bfloat16


def pairs(count, distance, phase):
    out = []
    for i in range(count):
        j = i + distance if (i // distance) % 2 == phase else i - distance
        if 0 <= j < count:
            out.append((i, j))
    return out


def plus(*terms):
    terms = [t for t in terms if t is not None]
    out = terms[0]
    for t in terms[1:]:
        out = out + t
    return out


def pick(values, k):
    return values[k] if 0 <= k < len(values) else None


def split(x):
    hi = x.astype(BF16)
    return hi, (x - hi.astype(F32)).astype(BF16)


def smooths(local, table, planes):
    hi, lo = split(jnp.concatenate(planes, 0))
    y = jnp.dot(table[...], hi, preferred_element_type=F32)
    z = jnp.dot(table[: 8 * SCALES_NU * local], lo, preferred_element_type=F32)
    out = []
    for s in range(SCALES_NU):
        row = []
        for k in range(local):
            at = 8 * (s * local + k)
            v = y[at : at + 8] + z[at : at + 8]
            if s == SCALES_NU - 1:
                v = v + y[at + 8 * local : at + 8 * local + 8]
            row.append(v)
        out.append(row)
    return out


def spectral_kernel(rows, cols, local, here, near, two_a, two_b, far_hi, far_lo, here2, near2, two_a2, two_b2, table, detail):
    me = lax.axis_index("chan").astype(jnp.int32)
    half = local // 2
    edge_a = half * ((me // 4) % 2)
    edge_b = half - edge_a
    for g in range(rows // 8):
        r = pl.ds(8 * g, 8)
        planes = [here[k, r] for k in range(local)] + [near[k, r] for k in range(local)]
        planes += [two_a[edge_a + k, r] for k in range(half)] + [two_b[edge_b + k, r] for k in range(half)]
        planes += [far_hi[k, r] for k in range(half)] + [far_lo[k, r] for k in range(half)]
        for ref in (here2, near2, two_a2, two_b2):
            planes += [ref[k, r] for k in range(local)]
        e = [planes[:local]] + smooths(local, table, planes)
        for k in range(local):
            for s in range(SCALES_NU + 1):
                d = e[s][k] - e[s + 1][k] if s < SCALES_NU else e[s][k]
                for h in range(cols // LANES):
                    detail[k, s, h, r] = d[:, h * LANES : (h + 1) * LANES]


def denoise_kernel(rows, cols, local, mult, noise, far_hi2, far_lo2, table, partial, mats, out, *scratch):
    detail, a, p, acc, done, out_sem = scratch
    halves = cols // LANES
    groups = rows // 8
    half = local // 2
    for s in range(SCALES_NU + 1):
        for h in range(halves):
            p[s, h, :EDGE] = jnp.zeros((EDGE, LANES), F32)
            p[s, h, EDGE + rows :] = jnp.zeros((EDGE, LANES), F32)
    for g in range(groups):
        r = pl.ds(8 * g, 8)
        e = smooths(local, table, [far_lo2[k, r] for k in range(half)] + [far_hi2[k, r] for k in range(half)])
        for k in range(local):
            for s in range(SCALES_NU + 1):
                if s == 0:
                    d = -e[0][k]
                else:
                    d = e[s - 1][k] - e[s][k] if s < SCALES_NU else e[s - 1][k]
                for h in range(halves):
                    detail[k, s, h, r] = partial[k, s, h, r] + d[:, h * LANES : (h + 1) * LANES]

    def spatial(i, carry):
        def limits(j, s):
            level = jnp.full((8, LANES), (mult[s, j] * noise[i, s, j]).astype(F32) * (1.0 / 1024.0))
            return -level, level

        def shrink(v, ends):
            return v - jnp.minimum(jnp.maximum(v, ends[0]), ends[1])

        def source(j, s):
            return detail.at[i, s] if j == 0 else a.at[s]

        def columns(j, s):
            src = source(j, s)
            hi, lo = split(jnp.concatenate([src[h] for h in range(halves)], 1))
            y = jnp.dot(jnp.concatenate([hi, lo], 0), mats[j], preferred_element_type=F32)
            y = y[:rows] + y[rows:]
            for h in range(halves):
                p[s, h, pl.ds(EDGE, rows)] = y[:, h * LANES : (h + 1) * LANES]

        def smooth_rows(j, s, h):
            d = 2**j

            def load(o):
                return [p[s, h, pl.ds(EDGE + 8 * k + o, 8)] for k in range(groups)]

            x = load(0)
            if d >= 8:
                q = d // 8
                cur = x
                for _ in range(4):
                    cur = [plus(pick(cur, k), pick(cur, k - q)) for k in range(len(cur) + q)]
                return cur[2 * q : 2 * q + groups]
            if d == 4:
                u = [p[s, h, pl.ds(EDGE + 8 * k - 4, 8)] for k in range(groups + 1)]
                near = [u[k] + u[k + 1] for k in range(groups)]
                far = [plus(pick(x, k - 1), pick(x, k + 1)) for k in range(groups)]
            elif d == 2:
                u = [p[s, h, pl.ds(EDGE + 8 * k - 4, 8)] for k in range(groups + 1)]
                near = [m + n for m, n in zip(load(-2), load(2))]
                far = [u[k] + u[k + 1] for k in range(groups)]
            else:
                near = [m + n for m, n in zip(load(-1), load(1))]
                far = [m + n for m, n in zip(load(-2), load(2))]
            return [6.0 * x[k] + 4.0 * near[k] + far[k] for k in range(groups)]

        for j in range(SCALES_XY):
            ends = [limits(j, s) for s in range(SCALES_NU + 1)]
            for s in range(SCALES_NU + 1):
                columns(j, s)
            for h in range(halves):
                total = [None] * groups
                for s in range(SCALES_NU + 1):
                    src = source(j, s)
                    y = smooth_rows(j, s, h)
                    for k in range(groups):
                        r = pl.ds(8 * k, 8)
                        v = shrink(src[h, r] - y[k], ends[s])
                        a[s, h, r] = y[k]
                        total[k] = plus(total[k], v)
                for k in range(groups):
                    r = pl.ds(8 * k, 8)
                    if j == 0:
                        acc[h, r] = total[k]
                    else:
                        acc[h, r] += total[k]
        ends = [limits(SCALES_XY, s) for s in range(SCALES_NU)]
        for h in range(halves):
            for k in range(groups):
                r = pl.ds(8 * k, 8)
                total = acc[h, r] + a[SCALES_NU, h, r]
                for s in range(SCALES_NU):
                    total = total + shrink(a[s, h, r], ends[s])
                done[i, r, h * LANES : (h + 1) * LANES] = total
        pltpu.make_async_copy(done.at[i], out.at[i], out_sem.at[i]).start()
        return carry

    lax.fori_loop(0, local, spatial, 0)
    for i in range(local):
        pltpu.make_async_copy(done.at[i], out.at[i], out_sem.at[i]).wait()


def places(i, local):
    beside = 1 - 2 * (i % 2)
    up2 = 2 - 4 * (i // 2 % 2)
    up4 = 4 - 8 * (i // 4 % 2)
    half = local // 2

    def block(at, lo=0, hi=local):
        return [at * local + o for o in range(lo, hi)]

    def edge(at):
        return block(at, half) if at < 0 else block(at, 0, half)

    early = block(0) + block(up2) + edge(up4) + edge(-up4) + block(-up2, half) + block(-up2, 0, half)
    for at in (0, up2, up4, -up4):
        early += block(at + beside)
    return early, block(-up2 + beside)


def spectral_tables(count, local):
    n = count * local
    whole = np.eye(n)
    parts = []
    for s in range(SCALES_NU):
        whole = sum(w / 16.0 * np.eye(n, k=(k - 2) * 2**s) for k, w in enumerate(TAPS)) @ whole
        parts.append(whole)
    hi = parts[-1].astype(BF16).astype(np.float64)
    parts[-1:] = [hi, parts[-1] - hi]
    tables = [], []
    for i in range(count):
        own = np.concatenate([p[i * local : (i + 1) * local] for p in parts])
        both = places(i, local)
        seen = [at for at in both[0] + both[1] if -REACH <= at < local + REACH]
        assert sorted(seen) == list(range(-REACH, local + REACH))
        for table, held in zip(tables, both):
            taps = np.zeros((own.shape[0], len(held)))
            for c, at in enumerate(held):
                if 0 <= i * local + at < n:
                    taps[:, c] = own[:, i * local + at]
            table.append(np.kron(taps, np.eye(8)))
    return [jnp.asarray(np.stack(t), BF16) for t in tables]


def setup_kernel(cols, cube, here, mats, sem):
    fetch = pltpu.make_async_copy(cube, here, sem)
    fetch.start()
    row = lax.broadcasted_iota(jnp.int32, (cols, cols), 0)
    offset = lax.broadcasted_iota(jnp.int32, (cols, cols), 1) - row
    for j in range(SCALES_XY):
        m = jnp.zeros((cols, cols), F32)
        for k, w in enumerate(TAPS):
            m = jnp.where(offset == (k - 2) * 2**j, w / 256.0, m)
        mats[j] = m.astype(BF16)
    fetch.wait()


def per_device(count, cube, multipliers, noise_code):
    local, rows, cols = cube.shape
    assert local == 4 and count % 8 == 0 and rows % 8 == 0 and cols % LANES == 0
    smem = pl.BlockSpec(memory_space=pltpu.SMEM)
    hbm = pl.BlockSpec(memory_space=pltpu.HBM)
    vmem = pl.BlockSpec(memory_space=pltpu.VMEM)
    anyspace = pl.BlockSpec(memory_space=pl.ANY)

    def permute(v, distance, phase):
        return lax.ppermute(v, "chan", pairs(count, distance, phase))

    relay = [(i, i + 4) for i in range(count - 4) if (i // 2) % 2 == 0]
    relay += [(i, i - 4) for i in range(4, count) if (i // 2) % 2 == 1]
    cut = local // 2
    near = permute(cube, 2, 0)
    two_a = permute(cube, 4, 0)
    two_b = permute(cube, 4, 1)
    me = lax.axis_index("chan")
    early, late = [lax.dynamic_index_in_dim(t, me, 0, False) for t in spectral_tables(count, local)]
    upper, early, late = lax.optimization_barrier((cube[cut:], early, late))
    far_hi = permute(upper, 2, 1)
    far_lo = lax.ppermute(near[:cut], "chan", relay)
    here, mats = pl.pallas_call(
        functools.partial(setup_kernel, cols),
        in_specs=[anyspace],
        out_specs=[vmem] * 2,
        out_shape=[jax.ShapeDtypeStruct(cube.shape, F32), jax.ShapeDtypeStruct((SCALES_XY, cols, cols), BF16)],
        scratch_shapes=[pltpu.SemaphoreType.DMA],
        compiler_params=pltpu.CompilerParams(vmem_limit_bytes=4 * 2**20),
        cost_estimate=pl.CostEstimate(flops=10**7, bytes_accessed=2 * 10**6, transcendentals=0),
        name="setup",
    )(cube)
    two_a, two_b, near, here, mats = lax.optimization_barrier((two_a, two_b, near, here, mats))
    far_hi, far_lo = lax.optimization_barrier((far_hi, far_lo))
    pieces = [here, near, two_a, two_b, far_hi, far_lo]
    passed = [permute(cube if n == 0 else v, 1, 0) for n, v in enumerate(pieces)]
    plane = (cols // LANES, rows, LANES)
    scales = SCALES_NU + 1
    partial = pl.pallas_call(
        functools.partial(spectral_kernel, rows, cols, local),
        in_specs=[vmem] * 11,
        out_specs=vmem,
        out_shape=jax.ShapeDtypeStruct((local, scales) + plane, F32),
        compiler_params=pltpu.CompilerParams(vmem_limit_bytes=11 * 2**20),
        cost_estimate=pl.CostEstimate(flops=1, bytes_accessed=1, transcendentals=0),
        name="spectral",
    )(*pieces, *passed[:4], early)
    return pl.pallas_call(
        functools.partial(denoise_kernel, rows, cols, local),
        in_specs=[smem] * 2 + [vmem] * 5,
        out_specs=hbm,
        out_shape=jax.ShapeDtypeStruct(cube.shape, F32),
        scratch_shapes=[
            pltpu.VMEM((local, scales) + plane, F32),
            pltpu.VMEM((scales,) + plane, F32),
            pltpu.VMEM((scales, cols // LANES, rows + 2 * EDGE, LANES), F32),
            pltpu.VMEM(plane, F32),
            pltpu.VMEM((local, rows, cols), F32),
            pltpu.SemaphoreType.DMA((local,)),
        ],
        compiler_params=pltpu.CompilerParams(vmem_limit_bytes=11 * 2**20),
        name="denoise",
    )(multipliers.T, noise_code.transpose(0, 2, 1), *passed[4:], late, partial, mats)


def solution(mesh):
    placed = (P(("slab", "chan"), None, None), P(), P(("slab", "chan"), None, None))
    return jax.shard_map(
        functools.partial(per_device, mesh.shape["chan"]),
        mesh=mesh,
        in_specs=placed,
        out_specs=P(("slab", "chan"), None, None),
        check_vma=False,
    )
```

```python
import functools

import jax
import jax.numpy as jnp
import numpy as np
from jax import lax
from jax.experimental import pallas as pl
from jax.experimental.pallas import tpu as pltpu
from jax.sharding import PartitionSpec as P

SCALES_XY = 5
SCALES_NU = 3
TAPS = (1, 4, 6, 4, 1)
REACH = 14
LANES = 128
EDGE = 8
F32 = jnp.float32
BF16 = jnp.bfloat16


def pairs(count, distance, phase):
    out = []
    for i in range(count):
        j = i + distance if (i // distance) % 2 == phase else i - distance
        if 0 <= j < count:
            out.append((i, j))
    return out


def plus(*terms):
    terms = [t for t in terms if t is not None]
    out = terms[0]
    for t in terms[1:]:
        out = out + t
    return out


def pick(values, k):
    return values[k] if 0 <= k < len(values) else None


def split(x):
    hi = x.astype(BF16)
    return hi, (x - hi.astype(F32)).astype(BF16)


def smooths(local, table, planes):
    hi, lo = split(jnp.concatenate(planes, 0))
    y = jnp.dot(table[...], hi, preferred_element_type=F32)
    z = jnp.dot(table[: 8 * SCALES_NU * local], lo, preferred_element_type=F32)
    out = []
    for s in range(SCALES_NU):
        row = []
        for k in range(local):
            at = 8 * (s * local + k)
            v = y[at : at + 8] + z[at : at + 8]
            if s == SCALES_NU - 1:
                v = v + y[at + 8 * local : at + 8 * local + 8]
            row.append(v)
        out.append(row)
    return out


def spectral_kernel(rows, cols, local, here, near, two_a, two_b, far_hi, far_lo, here2, near2, two_a2, two_b2, table, detail):
    me = lax.axis_index("chan").astype(jnp.int32)
    half = local // 2
    edge_a = half * ((me // 4) % 2)
    edge_b = half - edge_a
    for g in range(rows // 8):
        r = pl.ds(8 * g, 8)
        planes = [here[k, r] for k in range(local)] + [near[k, r] for k in range(local)]
        planes += [two_a[edge_a + k, r] for k in range(half)] + [two_b[edge_b + k, r] for k in range(half)]
        planes += [far_hi[k, r] for k in range(half)] + [far_lo[k, r] for k in range(half)]
        for ref in (here2, near2, two_a2, two_b2):
            planes += [ref[k, r] for k in range(local)]
        e = [planes[:local]] + smooths(local, table, planes)
        for k in range(local):
            for s in range(SCALES_NU + 1):
                d = e[s][k] - e[s + 1][k] if s < SCALES_NU else e[s][k]
                for h in range(cols // LANES):
                    detail[k, s, h, r] = d[:, h * LANES : (h + 1) * LANES]


def denoise_kernel(rows, cols, local, mult, noise, far_hi2, far_lo2, table, partial, mats, out, *scratch):
    mult_s, noise_s, detail, a, p, acc, done, code_sem, out_sem = scratch
    codes = [
        pltpu.make_async_copy(mult, mult_s, code_sem.at[0]),
        pltpu.make_async_copy(noise, noise_s, code_sem.at[1]),
    ]
    for c in codes:
        c.start()
    halves = cols // LANES
    groups = rows // 8
    half = local // 2
    for s in range(SCALES_NU + 1):
        for h in range(halves):
            p[s, h, :EDGE] = jnp.zeros((EDGE, LANES), F32)
            p[s, h, EDGE + rows :] = jnp.zeros((EDGE, LANES), F32)
    for g in range(groups):
        r = pl.ds(8 * g, 8)
        e = smooths(local, table, [far_lo2[k, r] for k in range(half)] + [far_hi2[k, r] for k in range(half)])
        for k in range(local):
            for s in range(SCALES_NU + 1):
                if s == 0:
                    d = -e[0][k]
                else:
                    d = e[s - 1][k] - e[s][k] if s < SCALES_NU else e[s - 1][k]
                for h in range(halves):
                    detail[k, s, h, r] = partial[k, s, h, r] + d[:, h * LANES : (h + 1) * LANES]

    def spatial(i, carry):
        def limits(j, s):
            level = jnp.full((8, LANES), (mult_s[s, j] * noise_s[i, s, j]).astype(F32) * (1.0 / 1024.0))
            return -level, level

        def shrink(v, ends):
            return v - jnp.minimum(jnp.maximum(v, ends[0]), ends[1])

        def source(j, s):
            return detail.at[i, s] if j == 0 else a.at[s]

        def columns(j, s):
            src = source(j, s)
            hi, lo = split(jnp.concatenate([src[h] for h in range(halves)], 1))
            y = jnp.dot(jnp.concatenate([hi, lo], 0), mats[j], preferred_element_type=F32)
            y = y[:rows] + y[rows:]
            for h in range(halves):
                p[s, h, pl.ds(EDGE, rows)] = y[:, h * LANES : (h + 1) * LANES]

        def smooth_rows(j, s, h):
            d = 2**j

            def load(o):
                return [p[s, h, pl.ds(EDGE + 8 * k + o, 8)] for k in range(groups)]

            x = load(0)
            if d >= 8:
                q = d // 8
                cur = x
                for _ in range(4):
                    cur = [plus(pick(cur, k), pick(cur, k - q)) for k in range(len(cur) + q)]
                return cur[2 * q : 2 * q + groups]
            if d == 4:
                u = [p[s, h, pl.ds(EDGE + 8 * k - 4, 8)] for k in range(groups + 1)]
                near = [u[k] + u[k + 1] for k in range(groups)]
                far = [plus(pick(x, k - 1), pick(x, k + 1)) for k in range(groups)]
            elif d == 2:
                u = [p[s, h, pl.ds(EDGE + 8 * k - 4, 8)] for k in range(groups + 1)]
                near = [m + n for m, n in zip(load(-2), load(2))]
                far = [u[k] + u[k + 1] for k in range(groups)]
            else:
                near = [m + n for m, n in zip(load(-1), load(1))]
                far = [m + n for m, n in zip(load(-2), load(2))]
            return [6.0 * x[k] + 4.0 * near[k] + far[k] for k in range(groups)]

        for j in range(SCALES_XY):
            ends = [limits(j, s) for s in range(SCALES_NU + 1)]
            for s in range(SCALES_NU + 1):
                columns(j, s)
            for h in range(halves):
                total = [None] * groups
                for s in range(SCALES_NU + 1):
                    src = source(j, s)
                    y = smooth_rows(j, s, h)
                    for k in range(groups):
                        r = pl.ds(8 * k, 8)
                        v = shrink(src[h, r] - y[k], ends[s])
                        a[s, h, r] = y[k]
                        total[k] = plus(total[k], v)
                for k in range(groups):
                    r = pl.ds(8 * k, 8)
                    if j == 0:
                        acc[h, r] = total[k]
                    else:
                        acc[h, r] += total[k]
        ends = [limits(SCALES_XY, s) for s in range(SCALES_NU)]
        for h in range(halves):
            for k in range(groups):
                r = pl.ds(8 * k, 8)
                total = acc[h, r] + a[SCALES_NU, h, r]
                for s in range(SCALES_NU):
                    total = total + shrink(a[s, h, r], ends[s])
                done[i, r, h * LANES : (h + 1) * LANES] = total
        pltpu.make_async_copy(done.at[i], out.at[i], out_sem.at[i]).start()
        return carry

    for c in codes:
        c.wait()
    lax.fori_loop(0, local, spatial, 0)
    for i in range(local):
        pltpu.make_async_copy(done.at[i], out.at[i], out_sem.at[i]).wait()


def places(i, local):
    beside = 1 - 2 * (i % 2)
    up2 = 2 - 4 * (i // 2 % 2)
    up4 = 4 - 8 * (i // 4 % 2)
    half = local // 2

    def block(at, lo=0, hi=local):
        return [at * local + o for o in range(lo, hi)]

    def edge(at):
        return block(at, half) if at < 0 else block(at, 0, half)

    early = block(0) + block(up2) + edge(up4) + edge(-up4) + block(-up2, half) + block(-up2, 0, half)
    for at in (0, up2, up4, -up4):
        early += block(at + beside)
    return early, block(-up2 + beside)


def spectral_tables(count, local):
    n = count * local
    whole = np.eye(n)
    parts = []
    for s in range(SCALES_NU):
        whole = sum(w / 16.0 * np.eye(n, k=(k - 2) * 2**s) for k, w in enumerate(TAPS)) @ whole
        parts.append(whole)
    hi = parts[-1].astype(BF16).astype(np.float64)
    parts[-1:] = [hi, parts[-1] - hi]
    tables = [], []
    for i in range(count):
        own = np.concatenate([p[i * local : (i + 1) * local] for p in parts])
        both = places(i, local)
        seen = [at for at in both[0] + both[1] if -REACH <= at < local + REACH]
        assert sorted(seen) == list(range(-REACH, local + REACH))
        for table, held in zip(tables, both):
            taps = np.zeros((own.shape[0], len(held)))
            for c, at in enumerate(held):
                if 0 <= i * local + at < n:
                    taps[:, c] = own[:, i * local + at]
            table.append(np.kron(taps, np.eye(8)))
    return [jnp.asarray(np.stack(t), BF16) for t in tables]


def setup_kernel(cols, cube, here, mats, sem):
    fetch = pltpu.make_async_copy(cube, here, sem)
    fetch.start()
    row = lax.broadcasted_iota(jnp.int32, (cols, cols), 0)
    offset = lax.broadcasted_iota(jnp.int32, (cols, cols), 1) - row
    for j in range(SCALES_XY):
        m = jnp.zeros((cols, cols), F32)
        for k, w in enumerate(TAPS):
            m = jnp.where(offset == (k - 2) * 2**j, w / 256.0, m)
        mats[j] = m.astype(BF16)
    fetch.wait()


def per_device(count, cube, multipliers, noise_code):
    local, rows, cols = cube.shape
    assert local == 4 and count % 8 == 0 and rows % 8 == 0 and cols % LANES == 0
    hbm = pl.BlockSpec(memory_space=pltpu.HBM)
    vmem = pl.BlockSpec(memory_space=pltpu.VMEM)
    anyspace = pl.BlockSpec(memory_space=pl.ANY)

    def permute(v, distance, phase):
        return lax.ppermute(v, "chan", pairs(count, distance, phase))

    relay = [(i, i + 4) for i in range(count - 4) if (i // 2) % 2 == 0]
    relay += [(i, i - 4) for i in range(4, count) if (i // 2) % 2 == 1]
    cut = local // 2
    near = permute(cube, 2, 0)
    two_a = permute(cube, 4, 0)
    two_b = permute(cube, 4, 1)
    me = lax.axis_index("chan")
    early, late = [lax.dynamic_index_in_dim(t, me, 0, False) for t in spectral_tables(count, local)]
    upper, early, late = lax.optimization_barrier((cube[cut:], early, late))
    far_hi = permute(upper, 2, 1)
    far_lo = lax.ppermute(near[:cut], "chan", relay)
    here, mats = pl.pallas_call(
        functools.partial(setup_kernel, cols),
        in_specs=[anyspace],
        out_specs=[vmem] * 2,
        out_shape=[jax.ShapeDtypeStruct(cube.shape, F32), jax.ShapeDtypeStruct((SCALES_XY, cols, cols), BF16)],
        scratch_shapes=[pltpu.SemaphoreType.DMA],
        compiler_params=pltpu.CompilerParams(vmem_limit_bytes=4 * 2**20),
        cost_estimate=pl.CostEstimate(flops=10**7, bytes_accessed=2 * 10**6, transcendentals=0),
        name="setup",
    )(cube)
    two_a, two_b, near, here, mats = lax.optimization_barrier((two_a, two_b, near, here, mats))
    far_hi, far_lo = lax.optimization_barrier((far_hi, far_lo))
    pieces = [here, near, two_a, two_b, far_hi, far_lo]
    passed = [permute(cube if n == 0 else v, 1, 0) for n, v in enumerate(pieces)]
    plane = (cols // LANES, rows, LANES)
    scales = SCALES_NU + 1
    partial = pl.pallas_call(
        functools.partial(spectral_kernel, rows, cols, local),
        in_specs=[vmem] * 11,
        out_specs=vmem,
        out_shape=jax.ShapeDtypeStruct((local, scales) + plane, F32),
        compiler_params=pltpu.CompilerParams(vmem_limit_bytes=11 * 2**20),
        cost_estimate=pl.CostEstimate(flops=1, bytes_accessed=1, transcendentals=0),
        name="spectral",
    )(*pieces, *passed[:4], early)
    return pl.pallas_call(
        functools.partial(denoise_kernel, rows, cols, local),
        in_specs=[anyspace] * 2 + [vmem] * 5,
        out_specs=hbm,
        out_shape=jax.ShapeDtypeStruct(cube.shape, F32),
        scratch_shapes=[
            pltpu.SMEM((scales, SCALES_XY + 1), jnp.int32),
            pltpu.SMEM((local, scales, SCALES_XY + 1), jnp.int32),
            pltpu.VMEM((local, scales) + plane, F32),
            pltpu.VMEM((scales,) + plane, F32),
            pltpu.VMEM((scales, cols // LANES, rows + 2 * EDGE, LANES), F32),
            pltpu.VMEM(plane, F32),
            pltpu.VMEM((local, rows, cols), F32),
            pltpu.SemaphoreType.DMA((2,)),
            pltpu.SemaphoreType.DMA((local,)),
        ],
        compiler_params=pltpu.CompilerParams(vmem_limit_bytes=11 * 2**20),
        name="denoise",
    )(multipliers.T, noise_code.transpose(0, 2, 1), *passed[4:], late, partial, mats)


def solution(mesh):
    placed = (P(("slab", "chan"), None, None), P(), P(("slab", "chan"), None, None))
    return jax.shard_map(
        functools.partial(per_device, mesh.shape["chan"]),
        mesh=mesh,
        in_specs=placed,
        out_specs=P(("slab", "chan"), None, None),
        check_vma=False,
    )
```

```python
import functools

import jax
import jax.numpy as jnp
import numpy as np
from jax import lax
from jax.experimental import pallas as pl
from jax.experimental.pallas import tpu as pltpu
from jax.sharding import PartitionSpec as P

SCALES_XY = 5
SCALES_NU = 3
TAPS = (1, 4, 6, 4, 1)
REACH = 14
LANES = 128
EDGE = 8
F32 = jnp.float32
BF16 = jnp.bfloat16


def pairs(count, distance, phase):
    out = []
    for i in range(count):
        j = i + distance if (i // distance) % 2 == phase else i - distance
        if 0 <= j < count:
            out.append((i, j))
    return out


def plus(*terms):
    terms = [t for t in terms if t is not None]
    out = terms[0]
    for t in terms[1:]:
        out = out + t
    return out


def pick(values, k):
    return values[k] if 0 <= k < len(values) else None


def split(x):
    hi = x.astype(BF16)
    return hi, (x - hi.astype(F32)).astype(BF16)


def smooths(local, count, table, planes):
    hi, lo = split(jnp.concatenate(planes, 0))
    y = jnp.dot(table[...], hi, preferred_element_type=F32)
    z = jnp.dot(table[: 8 * count * local], lo, preferred_element_type=F32)
    out = []
    for s in range(count):
        row = []
        for k in range(local):
            at = 8 * (s * local + k)
            v = y[at : at + 8] + z[at : at + 8]
            if s == SCALES_NU - 1:
                v = v + y[at + 8 * local : at + 8 * local + 8]
            row.append(v)
        out.append(row)
    return out


def spectral_kernel(rows, cols, local, here, near, two_a, two_b, far, relayed, here2, near2, two_a2, two_b2, table, detail):
    me = lax.axis_index("chan").astype(jnp.int32)
    half = local // 2
    edge_a = half * ((me // 4) % 2)
    edge_b = half - edge_a
    for g in range(rows // 8):
        r = pl.ds(8 * g, 8)
        planes = [here[k, r] for k in range(local)] + [near[k, r] for k in range(local)]
        planes += [two_a[edge_a + k, r] for k in range(half)] + [two_b[edge_b + k, r] for k in range(half)]
        planes += [far[k, r] for k in range(half)] + [relayed[k, r] for k in range(half)]
        for ref in (here2, near2, two_a2, two_b2):
            planes += [ref[k, r] for k in range(local)]
        e = [planes[:local]] + smooths(local, SCALES_NU, table, planes)
        for k in range(local):
            for s in range(SCALES_NU + 1):
                d = e[s][k] - e[s + 1][k] if s < SCALES_NU else e[s][k]
                for h in range(cols // LANES):
                    detail[k, s, h, r] = d[:, h * LANES : (h + 1) * LANES]


def fetch_codes(mult, noise, mult_s, noise_s, sem):
    copies = [pltpu.make_async_copy(mult, mult_s, sem.at[0]), pltpu.make_async_copy(noise, noise_s, sem.at[1])]
    for c in copies:
        c.start()
    return copies


def limits(mult_s, noise_s, i, j, s):
    level = jnp.full((8, LANES), (mult_s[s, j] * noise_s[i, s, j]).astype(F32) * (1.0 / 1024.0))
    return -level, level


def shrink(v, ends):
    return v - jnp.minimum(jnp.maximum(v, ends[0]), ends[1])


def clear_edges(rows, p):
    for n in range(p.shape[0]):
        for h in range(p.shape[1]):
            p[n, h, :EDGE] = jnp.zeros((EDGE, LANES), F32)
            p[n, h, EDGE + rows :] = jnp.zeros((EDGE, LANES), F32)


def smooth_rows(groups, d, p):
    def load(o):
        return [p[pl.ds(EDGE + 8 * k + o, 8)] for k in range(groups)]

    x = load(0)
    if d >= 8:
        q = d // 8
        cur = x
        for _ in range(4):
            cur = [plus(pick(cur, k), pick(cur, k - q)) for k in range(len(cur) + q)]
        return cur[2 * q : 2 * q + groups]
    if d == 4:
        u = [p[pl.ds(EDGE + 8 * k - 4, 8)] for k in range(groups + 1)]
        near = [u[k] + u[k + 1] for k in range(groups)]
        far = [plus(pick(x, k - 1), pick(x, k + 1)) for k in range(groups)]
    elif d == 2:
        u = [p[pl.ds(EDGE + 8 * k - 4, 8)] for k in range(groups + 1)]
        near = [m + n for m, n in zip(load(-2), load(2))]
        far = [u[k] + u[k + 1] for k in range(groups)]
    else:
        near = [m + n for m, n in zip(load(-1), load(1))]
        far = [m + n for m, n in zip(load(-2), load(2))]
    return [6.0 * x[k] + 4.0 * near[k] + far[k] for k in range(groups)]


def spatial(rows, cols, mats, a, p, sources, ends_of, sums, add):
    halves = cols // LANES
    groups = rows // 8
    for j in range(SCALES_XY):
        ends = [ends_of(n, j) for n in range(len(sources))]
        source = [src if j == 0 else a.at[n] for n, src in enumerate(sources)]
        for n, src in enumerate(source):
            hi, lo = split(jnp.concatenate([src[h] for h in range(halves)], 1))
            y = jnp.dot(jnp.concatenate([hi, lo], 0), mats[j], preferred_element_type=F32)
            y = y[:rows] + y[rows:]
            for h in range(halves):
                p[n, h, pl.ds(EDGE, rows)] = y[:, h * LANES : (h + 1) * LANES]
        for t, members in enumerate(sums):
            for h in range(halves):
                total = [None] * groups
                for n in members:
                    y = smooth_rows(groups, 2**j, p.at[n, h])
                    for k in range(groups):
                        r = pl.ds(8 * k, 8)
                        v = shrink(source[n][h, r] - y[k], ends[n])
                        a[n, h, r] = y[k]
                        total[k] = plus(total[k], v)
                for k in range(groups):
                    add(j, t, h, pl.ds(8 * k, 8), total[k])


def first_kernel(rows, cols, local, mult, noise, here, here2, table, mats, out, mult_s, noise_s, detail, a, p, sem):
    codes = fetch_codes(mult, noise, mult_s, noise_s, sem)
    clear_edges(rows, p)
    half = local // 2
    begin = half * (1 - lax.axis_index("chan").astype(jnp.int32) % 2)
    for g in range(rows // 8):
        r = pl.ds(8 * g, 8)
        e = smooths(half, 1, table, [ref[k, r] for ref in (here, here2) for k in range(local)])[0]
        for k in range(half):
            d = here[begin + k, r] - e[k]
            for h in range(cols // LANES):
                detail[k, h, r] = d[:, h * LANES : (h + 1) * LANES]
    for c in codes:
        c.wait()

    def add(j, t, h, r, v):
        if j == 0:
            out[t, h, r] = v
        else:
            out[t, h, r] += v

    def ends_of(n, j):
        return limits(mult_s, noise_s, begin + n, j, 0)

    spatial(rows, cols, mats, a, p, [detail.at[k] for k in range(half)], ends_of, [[k] for k in range(half)], add)
    for k in range(half):
        ends = ends_of(k, SCALES_XY)
        for h in range(cols // LANES):
            for g in range(rows // 8):
                r = pl.ds(8 * g, 8)
                out[k, h, r] += shrink(a[k, h, r], ends)


def denoise_kernel(rows, cols, local, mult, noise, far2, relayed2, table, partial, begun, mats, out, *scratch):
    mult_s, noise_s, detail, a, p, acc, done, sem, out_sem = scratch
    halves = cols // LANES
    half = local // 2
    core = lax.axis_index("chan").astype(jnp.int32) % 2
    codes = fetch_codes(mult, noise, mult_s, noise_s, sem)
    clear_edges(rows, p)
    for g in range(rows // 8):
        r = pl.ds(8 * g, 8)
        e = smooths(local, SCALES_NU, table, [ref[k, r] for ref in (far2, relayed2) for k in range(ref.shape[0])])
        for k in range(local):
            for s in range(SCALES_NU + 1):
                if s == 0:
                    d = -e[0][k]
                else:
                    d = e[s - 1][k] - e[s][k] if s < SCALES_NU else e[s - 1][k]
                for h in range(halves):
                    detail[k, s, h, r] = partial[k, s, h, r] + d[:, h * LANES : (h + 1) * LANES]
    for c in codes:
        c.wait()

    copies = []
    for begin, scales in ((half * core, range(SCALES_NU + 1)), (half * (1 - core), range(1, SCALES_NU + 1))):
        streams = [(k, s) for k in range(half) for s in scales]
        sums = [[n for n, (k, _) in enumerate(streams) if k == t] for t in range(half)]

        def add(j, t, h, r, v, partly=scales[0] > 0):
            if j > 0:
                acc[t, h, r] += v
            else:
                acc[t, h, r] = v + begun[t, h, r] if partly else v

        def ends_of(n, j, begin=begin, streams=streams):
            k, s = streams[n]
            return limits(mult_s, noise_s, begin + k, j, s)

        spatial(rows, cols, mats, a, p, [detail.at[begin + k, s] for k, s in streams], ends_of, sums, add)
        for t, members in enumerate(sums):
            ends = [ends_of(n, SCALES_XY) for n in members[:-1]]
            for h in range(halves):
                for g in range(rows // 8):
                    r = pl.ds(8 * g, 8)
                    total = acc[t, h, r] + a[members[-1], h, r]
                    for n, lim in zip(members, ends):
                        total = total + shrink(a[n, h, r], lim)
                    done[begin + t, r, h * LANES : (h + 1) * LANES] = total
            copy = pltpu.make_async_copy(done.at[begin + t], out.at[begin + t], out_sem.at[len(copies)])
            copy.start()
            copies.append(copy)
    for copy in copies:
        copy.wait()


def places(i, local):
    beside = 1 - 2 * (i % 2)
    up2 = 2 - 4 * (i // 2 % 2)
    up4 = 4 - 8 * (i // 4 % 2)
    half = local // 2

    def block(at):
        return [at * local + o for o in range(local)]

    def edge(at):
        return block(at)[half:] if at < 0 else block(at)[:half]

    def passed(held):
        return [c + beside * local for c in held]

    early = block(0) + block(up2) + edge(up4) + edge(-up4) + block(-up2)[half:] + block(-up2)[:half]
    for at in (0, up2, up4, -up4):
        early += passed(block(at))
    last = passed(block(-up2)[half:] + block(-up2)[:half])
    return early, last, block(0) + passed(block(0))


def spectral_tables(count, local):
    n = count * local
    whole = np.eye(n)
    parts = []
    for s in range(SCALES_NU):
        whole = sum(w / 16.0 * np.eye(n, k=(k - 2) * 2**s) for k, w in enumerate(TAPS)) @ whole
        parts.append(whole)
    hi = parts[-1].astype(BF16).astype(np.float64)
    parts[-1:] = [hi, parts[-1] - hi]
    tables = [], [], []
    for i in range(count):
        own = np.concatenate([p[i * local : (i + 1) * local] for p in parts])
        both = places(i, local)
        seen = [at for at in both[0] + both[1] if -REACH <= at < local + REACH]
        assert sorted(seen) == list(range(-REACH, local + REACH))
        for table, held in zip(tables, both):
            begin = local // 2 * (1 - i % 2) if table is tables[2] else 0
            taps = np.zeros((local // 2 if table is tables[2] else own.shape[0], len(held)))
            for c, at in enumerate(held):
                if 0 <= i * local + at < n:
                    taps[:, c] = own[begin : begin + taps.shape[0], i * local + at]
            table.append(np.kron(taps, np.eye(8)))
    return [jnp.asarray(np.stack(t), BF16) for t in tables]


def setup_kernel(cols, cube, here, mats, sem):
    fetch = pltpu.make_async_copy(cube, here, sem)
    fetch.start()
    row = lax.broadcasted_iota(jnp.int32, (cols, cols), 0)
    offset = lax.broadcasted_iota(jnp.int32, (cols, cols), 1) - row
    for j in range(SCALES_XY):
        m = jnp.zeros((cols, cols), F32)
        for k, w in enumerate(TAPS):
            m = jnp.where(offset == (k - 2) * 2**j, w / 256.0, m)
        mats[j] = m.astype(BF16)
    fetch.wait()


def per_device(count, cube, multipliers, noise_code):
    local, rows, cols = cube.shape
    assert local == 4 and count % 8 == 0 and rows % 8 == 0 and cols % LANES == 0
    hbm = pl.BlockSpec(memory_space=pltpu.HBM)
    vmem = pl.BlockSpec(memory_space=pltpu.VMEM)
    anyspace = pl.BlockSpec(memory_space=pl.ANY)

    def permute(v, distance, phase):
        return lax.ppermute(v, "chan", pairs(count, distance, phase))

    relay = [(i, i + 4) for i in range(count - 4) if (i // 2) % 2 == 0]
    relay += [(i, i - 4) for i in range(4, count) if (i // 2) % 2 == 1]
    half = local // 2
    me = lax.axis_index("chan")
    near = permute(cube, 2, 0)
    two_a = permute(cube, 4, 0)
    two_b = permute(cube, 4, 1)
    early, late, one = [lax.dynamic_index_in_dim(t, me, 0, False) for t in spectral_tables(count, local)]
    upper, early, late, one = lax.optimization_barrier((cube[half:], early, late, one))
    far = permute(upper, 2, 1)
    here, mats = pl.pallas_call(
        functools.partial(setup_kernel, cols),
        in_specs=[anyspace],
        out_specs=[vmem] * 2,
        out_shape=[jax.ShapeDtypeStruct(cube.shape, F32), jax.ShapeDtypeStruct((SCALES_XY, cols, cols), BF16)],
        scratch_shapes=[pltpu.SemaphoreType.DMA],
        compiler_params=pltpu.CompilerParams(vmem_limit_bytes=4 * 2**20),
        cost_estimate=pl.CostEstimate(flops=10**7, bytes_accessed=2 * 10**6, transcendentals=0),
        name="setup",
    )(cube)
    plane = (cols // LANES, rows, LANES)
    scales = SCALES_NU + 1
    codes = (multipliers.T, noise_code.transpose(0, 2, 1))
    code_scratch = [
        pltpu.SMEM((scales, SCALES_XY + 1), jnp.int32),
        pltpu.SMEM((local, scales, SCALES_XY + 1), jnp.int32),
    ]

    def planes(n):
        return [
            pltpu.VMEM((n,) + plane, F32),
            pltpu.VMEM((n, cols // LANES, rows + 2 * EDGE, LANES), F32),
        ]

    here2 = permute(cube, 1, 0)
    begun = pl.pallas_call(
        functools.partial(first_kernel, rows, cols, local),
        in_specs=[anyspace] * 2 + [vmem] * 4,
        out_specs=vmem,
        out_shape=jax.ShapeDtypeStruct((half,) + plane, F32),
        scratch_shapes=code_scratch
        + [pltpu.VMEM((half,) + plane, F32)]
        + planes(half)
        + [pltpu.SemaphoreType.DMA((2,))],
        compiler_params=pltpu.CompilerParams(vmem_limit_bytes=4 * 2**20),
        cost_estimate=pl.CostEstimate(flops=10**7, bytes_accessed=2 * 10**6, transcendentals=0),
        name="first",
    )(*codes, here, here2, one, mats)
    relayed = lax.ppermute(near[:half], "chan", relay)
    two_a, two_b, near, here, mats = lax.optimization_barrier((two_a, two_b, near, here, mats))
    far, relayed, begun = lax.optimization_barrier((far, relayed, begun))
    near2, two_a2, two_b2, far2, relayed2 = [permute(v, 1, 0) for v in (near, two_a, two_b, far, relayed)]
    partial = pl.pallas_call(
        functools.partial(spectral_kernel, rows, cols, local),
        in_specs=[vmem] * 11,
        out_specs=vmem,
        out_shape=jax.ShapeDtypeStruct((local, scales) + plane, F32),
        compiler_params=pltpu.CompilerParams(vmem_limit_bytes=6 * 2**20),
        cost_estimate=pl.CostEstimate(flops=1, bytes_accessed=1, transcendentals=0),
        name="spectral",
    )(here, near, two_a, two_b, far, relayed, here2, near2, two_a2, two_b2, early)
    return pl.pallas_call(
        functools.partial(denoise_kernel, rows, cols, local),
        in_specs=[anyspace] * 2 + [vmem] * 6,
        out_specs=hbm,
        out_shape=jax.ShapeDtypeStruct(cube.shape, F32),
        scratch_shapes=code_scratch
        + [pltpu.VMEM((local, scales) + plane, F32)]
        + planes(half * scales)
        + [
            pltpu.VMEM((half,) + plane, F32),
            pltpu.VMEM((local, rows, cols), F32),
            pltpu.SemaphoreType.DMA((2,)),
            pltpu.SemaphoreType.DMA((local,)),
        ],
        compiler_params=pltpu.CompilerParams(vmem_limit_bytes=11 * 2**20),
        name="denoise",
    )(*codes, far2, relayed2, late, partial, begun, mats)


def solution(mesh):
    placed = (P(("slab", "chan"), None, None), P(), P(("slab", "chan"), None, None))
    return jax.shard_map(
        functools.partial(per_device, mesh.shape["chan"]),
        mesh=mesh,
        in_specs=placed,
        out_specs=P(("slab", "chan"), None, None),
        check_vma=False,
    )
```
